32 devices in a mesh: groups: 2 (over x), seq: 16 (over z, y, core).
Axes of the slice: x: 2, y: 2, z: 4, core: 2. Of those that a mesh axis runs over, the one named last changes fastest.
Arguments:
- tiles: bfloat16 [1024, 16, 1536], P(('groups', 'seq')), parts along dimension 0, may hold values from -6 to 6
- tile_gain: bfloat16 [1536], replicated, may hold values from 0.099609375 to 1.8984375
- w_query: bfloat16 [1536, 768], P('seq'), may hold values from -3 to 3
- w_key: bfloat16 [1536, 768], P('seq'), may hold values from -3 to 3
- w_value: bfloat16 [1536, 768], P('seq'), may hold values from -0.15625 to 0.15625
- w_out: bfloat16 [768, 1536], P('seq'), may hold values from -0.21875 to 0.21875
- pool_gain: bfloat16 [1536], replicated, may hold values from 0.099609375 to 1.8984375
- w_in: bfloat16 [1536, 768], P('seq'), may hold values from -0.15625 to 0.15625
- block_order: int32 [256], P('groups'), parts along dimension 0, may hold values from 0 to 127, each once
- slide_gain: bfloat16 [768], replicated, may hold values from 0.099609375 to 1.8984375
- w_sq: bfloat16 [768, 768], P('seq'), may hold values from -3 to 3
- w_sk: bfloat16 [768, 768], P('seq'), may hold values from -3 to 3
- w_sv: bfloat16 [768, 768], P('seq'), may hold values from -0.21875 to 0.21875
- w_so: bfloat16 [768, 768], P('seq'), may hold values from -0.21875 to 0.21875
Outputs:
- slide_out: bfloat16 [1024, 768], P(('groups', 'seq')), parts along dimension 0
The draws below stay inside these ranges and needn't reach their ends.
There are 2 independent parts, one for each index of `groups`. The reference program is written for one: setup_inputs(seed, part) draws one part's arguments, and reference() takes and returns one part's arrays. A program takes and returns all parts, laid end to end along the dimension named above; an argument that names none is the same for every part. Nothing has to cross between parts.
Inputs may be any that keep to these rules, and one draw needn't show every extreme that they name: block_order is a permutation of 0 to 127.
All inputs are finite; a program needn't handle non-finite values.
Results may differ from the reference program's by a relative error of at most 0.0085.
Values may be sent and summed in bfloat16 or wider, within the bound.
A program may use at most 128 MiB of HBM per device.

```python
import jax
import jax.numpy as jnp
from jax import lax

D = 1536
HT = 12
HD = 64
HS = 12
PATCHES = 16
BLK = 4
TA = 768
DS = 768
TILES = 512
NBLK = 128
SEG1 = 128
SEG2 = 256
SEG3 = 512


def shared_rows(key, salt, rows, columns):
    return jax.random.normal(jax.random.fold_in(key, salt), (rows, columns), jnp.float32) * rows ** (-0.5)


def coupled_key(key, rows, columns):
    own_part = jax.random.normal(key, (rows, columns), jnp.float32) * rows ** (-0.5)
    value = own_part
    return jnp.clip(value, -3.0, 3.0)


def draw_w_query(key, part):
    shared = shared_rows(key, 11, D, TA)
    return jnp.clip(shared, -3.0, 3.0).astype(jnp.bfloat16)


def draw_w_key(key, part):
    key = jax.random.fold_in(key, 4)
    return coupled_key(key, D, TA).astype(jnp.bfloat16)


def draw_w_sq(key, part):
    shared = shared_rows(key, 12, DS, DS)
    return jnp.clip(shared, -3.0, 3.0).astype(jnp.bfloat16)


def draw_w_sk(key, part):
    key = jax.random.fold_in(key, 6)
    return coupled_key(key, DS, DS).astype(jnp.bfloat16)


def shard_levels(stream_key, shape, split, low, largest):
    def one(dim, parts):
        steps = jax.random.uniform(jax.random.fold_in(jax.random.fold_in(stream_key, 6), dim), (parts,), jnp.float32, low / len(split), largest / len(split))
        return jnp.repeat(jnp.exp(steps), shape[dim] // parts).reshape((-1,) + (1,) * (len(shape) - dim - 1))

    loudness = one(*split[0])
    for cut in split[1:]:
        loudness = loudness * one(*cut)
    return loudness


def noise(rng, dims, deviation, reach, shards=(), kind=jnp.bfloat16):
    array = deviation * jax.random.normal(rng, dims, jnp.float32)
    if shards:
        array = array * shard_levels(rng, dims, shards, -0.22, 0.18)
    return jnp.clip(array, -reach, reach).astype(kind)


def setup_inputs(seed: int = 0, part: int = 0) -> dict:
    streams_of = jax.random.split(jax.random.key(seed), 15)
    part_keys = jax.random.split(jax.random.fold_in(streams_of[14], part), 15)
    tiles = noise(part_keys[0], (TILES, PATCHES, D), 1.0, 6.0, ((0, 16),))
    tile_gain = jnp.clip(1.0 + 0.18 * jax.random.normal(streams_of[1], (D,), jnp.float32), 0.099609375, 1.8984375).astype(jnp.bfloat16)
    w_query = draw_w_query(jax.random.fold_in(streams_of[14], 71), part)
    w_key = draw_w_key(jax.random.fold_in(streams_of[14], 71), part)
    w_value = noise(streams_of[4], (D, TA), D ** -0.5, 0.15625, ((0, 16),))
    w_out = noise(streams_of[5], (TA, D), TA ** -0.5, 0.21875, ((0, 16),))
    pool_gain = jnp.clip(1.0 + 0.18 * jax.random.normal(streams_of[6], (D,), jnp.float32), 0.099609375, 1.8984375).astype(jnp.bfloat16)
    w_in = noise(streams_of[7], (D, DS), D ** -0.5, 0.15625, ((0, 16),))
    block_order = jax.random.permutation(part_keys[8], NBLK).astype(jnp.int32)
    slide_gain = jnp.clip(1.0 + 0.18 * jax.random.normal(streams_of[9], (DS,), jnp.float32), 0.099609375, 1.8984375).astype(jnp.bfloat16)
    w_sq = draw_w_sq(jax.random.fold_in(streams_of[14], 71), part)
    w_sk = draw_w_sk(jax.random.fold_in(streams_of[14], 71), part)
    w_sv = noise(streams_of[12], (DS, DS), DS ** -0.5, 0.21875, ((0, 16),))
    w_so = noise(streams_of[13], (DS, DS), DS ** -0.5, 0.21875, ((0, 16),))
    return {"tiles": tiles, "tile_gain": tile_gain, "w_query": w_query, "w_key": w_key, "w_value": w_value, "w_out": w_out, "pool_gain": pool_gain, "w_in": w_in, "block_order": block_order, "slide_gain": slide_gain, "w_sq": w_sq, "w_sk": w_sk, "w_sv": w_sv, "w_so": w_so}


epsilon = 1e-06
scaling = 0.125

def norm_rows(rows, gain):
    values = rows.astype(jnp.float32)
    centred = values - lax.optimization_barrier(jnp.mean(values, axis=-1, keepdims=True))
    spread = lax.optimization_barrier(jnp.mean(centred * centred, axis=-1, keepdims=True))
    return centred * lax.rsqrt(spread + epsilon) * gain.astype(jnp.float32)

def kept_rounded(matrix):
    return lax.optimization_barrier(matrix.astype(jnp.bfloat16)).astype(jnp.float32)

def embed_tiles(tile_block, tile_gain, w_query, w_key, w_value, w_out, pool_gain, w_in):
    tile_total = tile_block.shape[0]
    normed = norm_rows(tile_block, tile_gain).astype(jnp.bfloat16).reshape(tile_total * PATCHES, D)

    def project(weight):
        product = jnp.dot(normed, weight, preferred_element_type=jnp.float32)
        return kept_rounded(product).reshape(tile_total, PATCHES, HT, HD)
    tile_query = project(w_query)
    tile_keys = project(w_key)
    tile_values = project(w_value)
    scores = jnp.einsum('tqhd,tkhd->thqk', tile_query, tile_keys) * scaling
    row_max = lax.optimization_barrier(jnp.max(scores, axis=-1, keepdims=True))
    weights = jnp.exp(scores - row_max)
    totals = lax.optimization_barrier(jnp.sum(weights, axis=-1, keepdims=True))
    attended = jnp.einsum('thqk,tkhd->tqhd', kept_rounded(weights), tile_values)
    attended = attended / jnp.transpose(totals, (0, 2, 1, 3))
    attended = attended.astype(jnp.bfloat16).reshape(tile_total * PATCHES, TA)
    hidden = tile_block.astype(jnp.float32).reshape(tile_total * PATCHES, D)
    hidden = hidden + jnp.dot(attended, w_out, preferred_element_type=jnp.float32)
    pooled = lax.optimization_barrier(jnp.mean(hidden.reshape(tile_total, PATCHES, D), axis=1))
    pooled_norm = norm_rows(pooled, pool_gain).astype(jnp.bfloat16)
    return jnp.dot(pooled_norm, w_in, preferred_element_type=jnp.float32).astype(jnp.bfloat16)

def reference(tiles, tile_gain, w_query, w_key, w_value, w_out, pool_gain, w_in, block_order, slide_gain, w_sq, w_sk, w_sv, w_so):
    grouped = tiles.reshape(TILES // 32, 32, PATCHES, D)

    def one_group(tile_block):
        return embed_tiles(tile_block, tile_gain, w_query, w_key, w_value, w_out, pool_gain, w_in)
    embeddings = lax.map(one_group, grouped).reshape(TILES, DS)
    ordered = embeddings.reshape(NBLK, BLK, DS)[block_order].reshape(TILES, DS)
    normed = norm_rows(ordered, slide_gain).astype(jnp.bfloat16)

    def project(weight):
        product = jnp.dot(normed, weight, preferred_element_type=jnp.float32)
        return kept_rounded(product).reshape(TILES, HS, HD)
    slide_query = project(w_sq)
    slide_keys = project(w_sk)
    slide_values = project(w_sv)
    head_ids = jnp.arange(HS)
    level_outs = []
    level_lses = []
    level_masks = []
    for seg_len, dilation in ((SEG1, 1), (SEG2, 2), (SEG3, 4)):
        chosen = (jnp.arange(dilation)[:, None] == head_ids[None, :] % dilation).astype(jnp.float32)
        segments = TILES // seg_len
        picked = seg_len // dilation

        def select(rows):
            shaped = rows.reshape(segments, picked, dilation, HS, HD)
            return jnp.einsum('sjrhd,rh->sjhd', shaped, chosen)
        query_rows = select(slide_query)
        key_rows = select(slide_keys)
        value_rows = select(slide_values)
        scores = jnp.einsum('sqhd,skhd->shqk', query_rows, key_rows) * scaling
        row_max = lax.optimization_barrier(jnp.max(scores, axis=-1, keepdims=True))
        weights = jnp.exp(scores - row_max)
        totals = lax.optimization_barrier(jnp.sum(weights, axis=-1, keepdims=True))
        level_out = jnp.einsum('shqk,skhd->sqhd', kept_rounded(weights), value_rows)
        level_out = level_out / jnp.transpose(totals, (0, 2, 1, 3))
        level_lse = jnp.transpose((row_max + jnp.log(totals))[..., 0], (0, 2, 1))
        level_outs.append(jnp.einsum('sjhd,rh->sjrhd', level_out, chosen).reshape(TILES, HS, HD))
        level_lses.append(jnp.einsum('sjh,rh->sjrh', level_lse, chosen).reshape(TILES, HS))
        level_masks.append(jnp.broadcast_to(chosen[None, None], (segments, picked, dilation, HS)).reshape(TILES, HS))
    stacked_lse = jnp.stack(level_lses)
    stacked_masks = jnp.stack(level_masks) > 0.5
    stacked_outs = jnp.stack(level_outs)
    best_lse = lax.optimization_barrier(jnp.max(jnp.where(stacked_masks, stacked_lse, -jnp.inf), axis=0))
    factors = jnp.where(stacked_masks, jnp.exp(stacked_lse - best_lse[None]), 0.0)
    mixed_heads = lax.optimization_barrier(jnp.sum(factors[..., None] * stacked_outs, axis=0)) / lax.optimization_barrier(jnp.sum(factors, axis=0))[..., None]
    mixed_heads = mixed_heads.astype(jnp.bfloat16).reshape(TILES, DS)
    result = ordered.astype(jnp.float32) + jnp.dot(mixed_heads, w_so, preferred_element_type=jnp.float32)
    return result.astype(jnp.bfloat16)
```

```python
import jax
import jax.numpy as jnp
from jax import lax
from jax.experimental import pallas as pl
from jax.experimental.pallas import tpu as pltpu
from jax.sharding import PartitionSpec as P

HT = 12
HD = 64
HS = 12


epsilon = 1e-06
scaling = 0.125


def partner(value, axis, apart):
    mask = 2**apart
    pairs = [(source, source ^ mask) for source in range(lax.axis_size(axis))]
    return lax.ppermute(value, axis, pairs)


def norm_rows(rows, gain):
    values = rows.astype(jnp.float32)
    centred = values - jnp.mean(values, axis=-1, keepdims=True)
    spread = jnp.mean(centred * centred, axis=-1, keepdims=True)
    return centred * lax.rsqrt(spread + epsilon) * gain.astype(jnp.float32)


def select_rows(rows, chosen, dilation):
    row_total, head_total, head_width = rows.shape
    grouped = rows.reshape(row_total // dilation, dilation, head_total, head_width)
    return jnp.sum(jnp.where(chosen[None, :, :, None], grouped, jnp.zeros((), rows.dtype)), axis=1)


def add_products(operands, shard_rows):
    return tuple(
        (
            jnp.dot(operand, weight_rows, preferred_element_type=jnp.float32)
            for operand, weight_rows in zip(operands, shard_rows)
        )
    )


def shards_by_gathers(
    tiles,
    tile_gain,
    w_query,
    w_key,
    w_value,
    w_out,
    pool_gain,
    w_in,
    block_order,
    slide_gain,
    w_sq,
    w_sk,
    w_sv,
    w_so,
):
    tile_count, patch_count, model_width = tiles.shape
    row_count = tile_count * patch_count
    inner_width = w_query.shape[1]
    normed = norm_rows(tiles, tile_gain).astype(jnp.bfloat16).reshape(row_count, model_width)
    projected = add_products(
        (normed, normed, normed),
        (
            lax.all_gather(w_query, "seq", axis=0, tiled=True),
            lax.all_gather(w_key, "seq", axis=0, tiled=True),
            lax.all_gather(w_value, "seq", axis=0, tiled=True),
        ),
    )
    tile_query, tile_keys, tile_values = (
        matrix.astype(jnp.bfloat16).reshape(tile_count, patch_count, HT, HD) for matrix in projected
    )
    scores = (
        jnp.einsum("tqhd,tkhd->thqk", tile_query, tile_keys, preferred_element_type=jnp.float32)
        * scaling
    )
    row_max = jnp.max(scores, axis=-1, keepdims=True)
    weights = jnp.exp(scores - row_max)
    totals = jnp.sum(weights, axis=-1)
    attended = jnp.einsum(
        "thqk,tkhd->tqhd",
        weights.astype(jnp.bfloat16),
        tile_values,
        preferred_element_type=jnp.float32,
    )
    attended = (attended / jnp.transpose(totals, (0, 2, 1))[..., None]).astype(jnp.bfloat16)
    attended_mean = jnp.mean(
        attended.reshape(tile_count, patch_count, inner_width), axis=1, dtype=jnp.float32
    )
    token_mean = jnp.mean(tiles, axis=1, dtype=jnp.float32)
    out_term = jnp.dot(
        attended_mean,
        lax.all_gather(w_out, "seq", axis=0, tiled=True).astype(jnp.float32),
        precision=lax.Precision.HIGHEST,
    )
    pooled = token_mean + out_term
    pooled_norm = norm_rows(pooled, pool_gain).astype(jnp.bfloat16)
    embedding = add_products((pooled_norm,), (lax.all_gather(w_in, "seq", axis=0, tiled=True),))[0]
    embedding = embedding.astype(jnp.bfloat16)
    position = lax.axis_index("seq")
    seq_size = lax.axis_size("seq")
    gathered = lax.all_gather(embedding, "seq", axis=0, tiled=True)
    slide_width = gathered.shape[1]
    block_count = block_order.shape[0]
    block_len = gathered.shape[0] // block_count
    blocks = gathered.reshape(block_count, block_len, slide_width)
    per_device = tile_count // block_len
    wanted = lax.dynamic_slice_in_dim(block_order, position * per_device, per_device)
    own_rows = jnp.take(blocks, wanted, axis=0).reshape(per_device * block_len, slide_width)
    own_norm = norm_rows(own_rows, slide_gain).astype(jnp.bfloat16)
    total_rows = seq_size * tile_count
    source_rows = own_norm.shape[0]
    slide_proj = add_products(
        (own_norm, own_norm, own_norm),
        (
            lax.all_gather(w_sq, "seq", axis=0, tiled=True),
            lax.all_gather(w_sk, "seq", axis=0, tiled=True),
            lax.all_gather(w_sv, "seq", axis=0, tiled=True),
        ),
    )
    slide_query = slide_proj[0].astype(jnp.bfloat16).reshape(tile_count, HS, HD)
    slide_keys = slide_proj[1].astype(jnp.bfloat16).reshape(source_rows, HS, HD)
    slide_values = slide_proj[2].astype(jnp.bfloat16).reshape(source_rows, HS, HD)
    head_ids = jnp.arange(HS)
    local_ids = jnp.arange(tile_count)
    level_outs = []
    level_lses = []
    level_masks = []
    for seg_len, dilation in ((total_rows // 4, 1), (total_rows // 2, 2), (total_rows, 4)):
        chosen = jnp.arange(dilation)[:, None] == head_ids[None, :] % dilation
        seg_keys = select_rows(slide_keys, chosen, dilation)
        seg_values = select_rows(slide_values, chosen, dilation)
        for bit_number in range((seg_len // tile_count).bit_length() - 1):
            other_keys, other_values = partner((seg_keys, seg_values), "seq", bit_number)
            low_half = position >> bit_number & 1 == 0
            seg_keys = jnp.where(
                low_half,
                jnp.concatenate([seg_keys, other_keys], 0),
                jnp.concatenate([other_keys, seg_keys], 0),
            )
            seg_values = jnp.where(
                low_half,
                jnp.concatenate([seg_values, other_values], 0),
                jnp.concatenate([other_values, seg_values], 0),
            )
        scores = (
            jnp.einsum("qhd,khd->hqk", slide_query, seg_keys, preferred_element_type=jnp.float32)
            * scaling
        )
        row_max = jnp.max(scores, axis=-1, keepdims=True)
        weights = jnp.exp(scores - row_max)
        totals = jnp.sum(weights, axis=-1)
        level_out = jnp.einsum(
            "hqk,khd->qhd",
            weights.astype(jnp.bfloat16),
            seg_values,
            preferred_element_type=jnp.float32,
        )
        level_outs.append(level_out / jnp.transpose(totals)[..., None])
        level_lses.append(jnp.transpose(row_max[..., 0] + jnp.log(totals)))
        level_masks.append(local_ids[:, None] % dilation == head_ids[None, :] % dilation)
    stacked_lse = jnp.stack(level_lses)
    stacked_masks = jnp.stack(level_masks)
    stacked_outs = jnp.stack(level_outs)
    best_lse = jnp.max(jnp.where(stacked_masks, stacked_lse, -jnp.inf), axis=0)
    factors = jnp.where(stacked_masks, jnp.exp(stacked_lse - best_lse[None]), 0.0)
    mixed_heads = (
        jnp.sum(factors[..., None] * stacked_outs, axis=0) / jnp.sum(factors, axis=0)[..., None]
    )
    mixed_heads = mixed_heads.astype(jnp.bfloat16).reshape(tile_count, slide_width)
    out_proj = add_products((mixed_heads,), (lax.all_gather(w_so, "seq", axis=0, tiled=True),))[0]
    return (own_rows.astype(jnp.float32) + out_proj).astype(jnp.bfloat16)


MESH = pl.DeviceIdType.MESH
f32, bf16 = jnp.float32, jnp.bfloat16


def iota(shape, dim):
    return lax.broadcasted_iota(jnp.int32, shape, dim)


def dot(a, b):
    return jnp.dot(a, b, preferred_element_type=f32)


def dot_t(a, b):
    return lax.dot_general(a, b, (((1,), (1,)), ((), ())), preferred_element_type=f32)


def attend(query, keys, values, mask=None):
    scores = dot_t(query, keys) * scaling
    if mask is not None:
        scores = jnp.where(mask, scores, -1e30)
    row_max = jnp.max(scores, axis=-1, keepdims=True)
    weights = jnp.exp(scores - row_max)
    if mask is not None:
        weights = jnp.where(mask, weights, 0.0)
    totals = jnp.sum(weights, axis=-1, keepdims=True)
    return dot(weights.astype(bf16), values) / totals, row_max + jnp.log(totals)


CHUNKS = (
    (0, 0, 384), (1, 0, 384), (2, 0, 384), (0, 384, 384), (1, 384, 384), (2, 384, 384),
    (3, 0, 768), (3, 768, 768), (4, 0, 384), (4, 384, 384), (5, 0, 768),
)
NCH = len(CHUNKS)
LINE = 4
SEQ = 16
LEAD = 2


def slab_kernel(
    tiles, tile_gain, w_query, w_key, w_value, w_out, pool_gain, w_in, block_order, slide_gain,
    w_sq, w_sk, w_sv, w_so, out,
    *scratch,
):
    bufs = scratch[:NCH]
    (normed, tq, tk, tv, att, emb, stage, wslide, perm, snorm, sq, sk, sv, souts, slses, mixp,
     msend, mrecv, mcat, own_rows,
     zs, zr, ys, yr, xs, xr, cs, cr, es, er, ws, wr, ms, mr) = scratch[NCH:]
    sources = (w_query, w_key, w_value, w_out, w_in, w_so)
    x = lax.axis_index("groups")
    me = lax.axis_index("seq")
    z = me // 4
    y = (me // 2) % 2
    c = me % 2
    at_y = {"seq": z * 4 + (1 - y) * 2 + c}
    at_c = {"seq": z * 4 + y * 2 + (1 - c)}
    at_x = {"groups": 1 - x}

    barrier = pltpu.get_barrier_semaphore()
    for o in range(1, SEQ):
        pl.semaphore_signal(barrier, inc=1, device_id={"seq": lax.rem(me + o, SEQ)}, device_id_type=MESH)
    pl.semaphore_signal(barrier, inc=1, device_id=at_x, device_id_type=MESH)

    for k, (w, first, cols) in enumerate(CHUNKS):
        bufs[k][z, y, c] = sources[w][:, first:first + cols]
    pl.semaphore_wait(barrier, SEQ)

    def copy(source, target, send, recv, device):
        return pltpu.make_async_remote_copy(
            src_ref=source, dst_ref=target, send_sem=send, recv_sem=recv,
            device_id=device, device_id_type=MESH,
        )

    def line_copy(k, way, s):
        block = z - (s - 1) if way == 0 else z + (s - 1)
        device = {"seq": me + 4} if way == 0 else {"seq": me - 4}
        valid = jnp.logical_and(z >= s - 1, z < LINE - 1) if way == 0 else jnp.logical_and(z <= LINE - s, z > 0)
        ref = bufs[k].at[block, y, c]
        n = way * 3 + s - 1
        return valid, copy(ref, ref, zs.at[k, n], zr.at[k, n], device)

    def line_send(k, s):
        for way in (0, 1):
            valid, remote = line_copy(k, way, s)
            pl.when(valid)(remote.start)

    def line_wait_send(k, s):
        for way in (0, 1):
            valid, remote = line_copy(k, way, s)
            pl.when(valid)(remote.wait_send)

    def line_wait(k, s):
        for way in (0, 1):
            valid = z >= s if way == 0 else z <= LINE - 1 - s
            block = z - s if way == 0 else z + s
            n = way * 3 + s - 1
            ref = bufs[k].at[block, y, c]
            pl.when(valid)(copy(ref, ref, zs.at[k, n], zr.at[k, n], {"seq": me}).wait_recv)

    def half(k, which_y, core, g):
        rows, cols = bufs[k].shape[3:]
        if rows % 32 == 0:
            return bufs[k].at[:, which_y, core, pl.ds(pl.multiple_of(g * (rows // 2), 16), rows // 2), :]
        return bufs[k].at[:, which_y, core, :, pl.ds(pl.multiple_of(g * (cols // 2), 128), cols // 2)]

    def y_copy(k):
        ref = half(k, y, c, x)
        return copy(ref, ref, ys.at[k], yr.at[k], at_y)

    def x_copy(k):
        ref = half(k, 1 - y, c, x)
        return copy(ref, ref, xs.at[k], xr.at[k], at_x)

    def c_copy(k, n):
        ref = bufs[k].at[:, y if n == 0 else 1 - y, c]
        return copy(ref, ref, cs.at[k, n], cr.at[k, n], at_c)

    def step(k, st):
        if st == 0:
            line_send(k, 1)
        elif st == 1:
            line_wait(k, 1)
            line_send(k, 2)
        elif st == 2:
            line_wait(k, 2)
            line_send(k, 3)
        elif st == 3:
            line_wait(k, 3)
            y_copy(k).start()
            c_copy(k, 0).start()
        elif st == 4:
            y_copy(k).wait_recv()
            x_copy(k).start()
        elif st == 5:
            x_copy(k).wait_recv()
            c_copy(k, 1).start()
        else:
            c_copy(k, 0).wait_recv()
            c_copy(k, 1).wait_recv()

    def tick(t):
        if t + LEAD < NCH:
            step(t + LEAD, 0)
        for st in range(6, 0, -1):
            if 0 <= t - st < NCH:
                step(t - st, st)

    def weight(k):
        rows, cols = bufs[k].shape[3:]
        return bufs[k][...].reshape(SEQ * rows, cols)

    def norm_piece(first, rows):
        @pl.loop(first, first + rows, step=64)
        def _(r):
            at = pl.ds(pl.multiple_of(r, 64), 64)
            normed[at, :] = norm_rows(tiles[at, :], tile_gain[...]).astype(bf16)

    def project(k, ref):
        @pl.loop(0, 512, step=128)
        def _(r):
            at = pl.ds(pl.multiple_of(r, 128), 128)
            ref[at, :] = dot(normed[at, :], weight(k)).astype(bf16)

    def tile_attention(part):
        mask = iota((128, 128), 0) // 16 == iota((128, 128), 1) // 16

        @pl.loop(0, 512, step=128)
        def _(r):
            at = pl.ds(pl.multiple_of(r, 128), 128)
            for pair in range(3):
                outs = []
                for h in (2 * pair, 2 * pair + 1):
                    cols = slice(h * 64, h * 64 + 64)
                    outs.append(attend(tq[at, cols], tk[at, cols], tv[at, cols], mask)[0])
                first = part * 384 + pair * 128
                att[at, first:first + 128] = jnp.concatenate(outs, axis=1).astype(bf16)

    def stage_slide():
        for h in range(HS):
            stage[h] = jnp.concatenate([w[:, h * 64:h * 64 + 64] for w in (w_sq, w_sk, w_sv)], axis=1)

        @pl.when(me < HS)
        def _():
            wslide[me] = stage[me]

    def w_copy(o, device, block):
        return copy(stage.at[block], wslide.at[me], ws.at[o], wr.at[o], {"seq": device})

    def slide_send(wait):
        for o in range(1, SEQ):
            d = lax.rem(me + o, SEQ)
            @pl.when(d < HS)
            def _():
                remote = w_copy(o, d, d)
                remote.wait_send() if wait else remote.start()

    def slide_wait():
        @pl.when(me < HS)
        def _():
            for o in range(1, SEQ):
                source = lax.rem(me + SEQ - o, SEQ)
                copy(stage.at[0], wslide.at[source], ws.at[o], wr.at[o], {"seq": me}).wait_recv()

    def source_rows(position):
        rows = position.shape[0]
        table = block_order[...].astype(f32)
        hot = iota((rows, 128), 1) == position[:, :1] // 4
        block = jnp.sum(jnp.where(hot, table, 0.0), axis=1, keepdims=True)
        source = block.astype(jnp.int32) * 4 + position[:, :1] % 4
        return (iota((rows, 512), 1) == source).astype(f32).astype(bf16)

    def build_perm():
        for j in range(4):
            perm[j * 128:j * 128 + 128, :] = source_rows(iota((128, 128), 0) * 4 + j)

    for k in range(LEAD):
        step(k, 0)
    done = {}
    for t in range(NCH + 6):
        tick(t)
        if t < 4:
            norm_piece(t * 128, 128)
        if t == 4:
            stage_slide()
        if t == 5:
            build_perm()
        if t == NCH - LEAD:
            slide_send(False)
        if t in (6, 9):
            project(t - 6, tq)
        if t in (7, 10):
            project(t - 6, tk)
        if t in (8, 11):
            project(t - 6, tv)
            tile_attention((t - 6) // 3)
        if t == 11:
            gather16 = (iota((32, 512), 1) // 16 == iota((32, 512), 0)).astype(f32).astype(bf16)
            token_mean = dot(gather16, tiles[...]) * (1.0 / 16.0)
            mean = dot(gather16, att[...]) * (1.0 / 16.0)
            high = mean.astype(bf16)
            low = (mean - high.astype(f32)).astype(bf16)
            both = jnp.concatenate([high, low], axis=0)
        if t in (12, 13):
            product = dot(both, weight(t - 6))
            done[t] = product[:32] + product[32:]
        if t == 13:
            pooled = token_mean + jnp.concatenate([done[12], done[13]], axis=1)
            pooled_norm = norm_rows(pooled, pool_gain[...]).astype(bf16)
        if t == 14:
            emb[z, y, c, :, :384] = dot(pooled_norm, weight(8)).astype(bf16)
        if t == 15:
            emb[z, y, c, :, 384:] = dot(pooled_norm, weight(9)).astype(bf16)
            def e_copy(n, d, ref):
                return copy(ref, ref, es.at[n], er.at[n], d)
            sends = []
            for o in range(1, LINE):
                sends.append(e_copy(o, {"seq": lax.rem(me + 4 * o, SEQ)}, emb.at[z, y, c]))
                sends[-1].start()
    for o in range(1, LINE):
        e_copy(o, {"seq": me}, emb.at[lax.rem(z + LINE - o, LINE), y, c]).wait_recv()
    to_y = e_copy(0, at_y, emb.at[:, y, c])
    to_y.start()
    to_c = e_copy(4, at_c, emb.at[:, y, c])
    to_c.start()
    slide_wait()
    to_y.wait_recv()
    to_c2 = e_copy(5, at_c, emb.at[:, 1 - y, c])
    to_c2.start()
    to_c.wait_recv()
    to_c2.wait_recv()

    every = emb[...].reshape(512, 768)
    own_rows[...] = dot(source_rows(iota((32, 128), 0) + me * 32), every)

    @pl.when(me < HS)
    def _():
        @pl.loop(0, 512, step=128)
        def _(r):
            at = pl.ds(pl.multiple_of(r, 128), 128)
            ordered = dot(perm[at, :], every)
            rows = norm_rows(ordered, slide_gain[...]).astype(bf16)
            projected = dot(rows, wslide[...].reshape(768, 192)).astype(bf16)
            sq[at, :] = projected[:, :64]
            sk[at, :] = projected[:, 64:128]
            sv[at, :] = projected[:, 128:]

        for level in (1, 2):
            slses[level] = jnp.full((512, 64), -1e30, f32)
            souts[level] = jnp.zeros((512, 64), f32)

        def level_attention(level, pieces):
            def rows(ref):
                return jnp.concatenate([ref[at, :] for at in pieces], axis=0)
            result, lse = attend(rows(sq), rows(sk), rows(sv))
            lse = jnp.broadcast_to(lse, result.shape)
            size = 128 // len(pieces)
            for n, at in enumerate(pieces):
                souts[level, at, :] = result[n * size:n * size + size]
                slses[level, at, :] = lse[n * size:n * size + size]

        for s in range(4):
            level_attention(0, [pl.ds(j * 128 + 32 * s, 32) for j in range(4)])
        even = (me % 2) * 128
        for s in range(2):
            level_attention(1, [pl.ds(pl.multiple_of(even + j * 256 + 64 * s, 64), 64) for j in range(2)])
        level_attention(2, [pl.ds(pl.multiple_of((me % 4) * 128, 128), 128)])
        best = jnp.maximum(jnp.maximum(slses[0], slses[1]), slses[2])
        total = jnp.zeros((512, 64), f32)
        mixed = jnp.zeros((512, 64), f32)
        for level in range(3):
            factor = jnp.exp(slses[level] - best)
            total = total + factor
            mixed = mixed + factor * souts[level]
        mixed = (mixed / total).astype(bf16)
        rows, cols = iota((512, 512), 0), iota((512, 512), 1)
        back = (cols == (rows % 4) * 128 + rows // 4).astype(f32).astype(bf16)
        msend[...] = dot(back, mixed).astype(bf16).reshape(SEQ, 32, 64)
        mrecv[me] = msend[me]
        for o in range(1, SEQ):
            d = lax.rem(me + o, SEQ)
            copy(msend.at[d], mrecv.at[me], ms.at[o], mr.at[o], {"seq": d}).start()

    for o in range(1, SEQ):
        source = lax.rem(me + SEQ - o, SEQ)
        pl.when(source < HS)(copy(msend.at[0], mrecv.at[jnp.minimum(source, HS - 1)], ms.at[o], mr.at[o], {"seq": me}).wait_recv)
    for h in range(HS):
        mcat[:, h * 64:h * 64 + 64] = mrecv[h]
    out[...] = (own_rows[...] + dot(mcat[...], weight(10))).astype(bf16)

    @pl.when(me < HS)
    def _():
        for o in range(1, SEQ):
            d = lax.rem(me + o, SEQ)
            copy(msend.at[d], mrecv.at[me], ms.at[o], mr.at[o], {"seq": d}).wait_send()
    slide_send(True)
    for remote in sends + [to_y, to_c, to_c2]:
        remote.wait_send()
    for k in range(NCH):
        for s in range(1, LINE):
            line_wait_send(k, s)
        y_copy(k).wait_send()
        x_copy(k).wait_send()
        c_copy(k, 0).wait_send()
        c_copy(k, 1).wait_send()


def shards_in_kernel(tiles, tile_gain, w_query, w_key, w_value, w_out, pool_gain, w_in, block_order,
                     slide_gain, w_sq, w_sk, w_sv, w_so):
    weights = (w_query, w_key, w_value, w_out, w_in, w_so)
    vmem, dma = pltpu.VMEM, pltpu.SemaphoreType.DMA
    scratch = [vmem((LINE, 2, 2, weights[w].shape[0], cols), bf16) for w, _, cols in CHUNKS]
    scratch += [
        vmem((512, 1536), bf16),
        vmem((512, 384), bf16), vmem((512, 384), bf16), vmem((512, 384), bf16),
        vmem((512, 768), bf16),
        vmem((LINE, 2, 2, 32, 768), bf16),
        vmem((HS, 48, 192), bf16), vmem((SEQ, 48, 192), bf16),
        vmem((512, 512), bf16),
        vmem((16, 128), bf16),
        vmem((512, 64), bf16), vmem((512, 64), bf16), vmem((512, 64), bf16),
        vmem((3, 512, 64), f32), vmem((3, 512, 64), f32),
        vmem((16, 128), bf16),
        vmem((SEQ, 32, 64), bf16), vmem((HS, 32, 64), bf16), vmem((32, 768), bf16),
        vmem((32, 768), f32),
        dma((NCH, 6)), dma((NCH, 6)), dma((NCH,)), dma((NCH,)), dma((NCH,)), dma((NCH,)),
        dma((NCH, 2)), dma((NCH, 2)), dma((6,)), dma((6,)),
        dma((SEQ,)), dma((SEQ,)), dma((SEQ,)), dma((SEQ,)),
    ]
    return pl.pallas_call(
        slab_kernel,
        out_shape=jax.ShapeDtypeStruct((32, 768), bf16),
        in_specs=[pl.BlockSpec(memory_space=pltpu.VMEM)] * 14,
        out_specs=pl.BlockSpec(memory_space=pltpu.VMEM),
        scratch_shapes=scratch,
        compiler_params=pltpu.CompilerParams(
            collective_id=0, has_side_effects=True, vmem_limit_bytes=56 * 1024 * 1024
        ),
        cost_estimate=pl.CostEstimate(flops=6 * 10**9, bytes_accessed=4 * 10**6, transcendentals=10**6),
        name="slab",
    )(
        tiles.reshape(512, 1536), tile_gain.reshape(1, -1), w_query, w_key, w_value, w_out,
        pool_gain.reshape(1, -1), w_in, block_order.reshape(1, -1), slide_gain.reshape(1, -1),
        w_sq, w_sk, w_sv, w_so,
    )


def solution(mesh):
    shards = shards_by_gathers
    if mesh.shape['groups'] == 2 and mesh.shape['seq'] == 16:
        shards = shards_in_kernel

    placed = (
        P(("groups", "seq"), None, None),
        P(),
        P("seq", None),
        P("seq", None),
        P("seq", None),
        P("seq", None),
        P(),
        P("seq", None),
        P("groups"),
        P(),
        P("seq", None),
        P("seq", None),
        P("seq", None),
        P("seq", None),
    )
    return jax.shard_map(
        shards, mesh=mesh, in_specs=placed, out_specs=P(("groups", "seq"), None), check_vma=False
    )
```

```python
import jax
import jax.numpy as jnp
from jax import lax
from jax.experimental import pallas as pl
from jax.experimental.pallas import tpu as pltpu
from jax.sharding import PartitionSpec as P

HT = 12
HD = 64
HS = 12


epsilon = 1e-06
scaling = 0.125


def partner(value, axis, apart):
    mask = 2**apart
    pairs = [(source, source ^ mask) for source in range(lax.axis_size(axis))]
    return lax.ppermute(value, axis, pairs)


def norm_rows(rows, gain):
    values = rows.astype(jnp.float32)
    centred = values - jnp.mean(values, axis=-1, keepdims=True)
    spread = jnp.mean(centred * centred, axis=-1, keepdims=True)
    return centred * lax.rsqrt(spread + epsilon) * gain.astype(jnp.float32)


def select_rows(rows, chosen, dilation):
    row_total, head_total, head_width = rows.shape
    grouped = rows.reshape(row_total // dilation, dilation, head_total, head_width)
    return jnp.sum(jnp.where(chosen[None, :, :, None], grouped, jnp.zeros((), rows.dtype)), axis=1)


def add_products(operands, shard_rows):
    return tuple(
        (
            jnp.dot(operand, weight_rows, preferred_element_type=jnp.float32)
            for operand, weight_rows in zip(operands, shard_rows)
        )
    )


def shards_by_gathers(
    tiles,
    tile_gain,
    w_query,
    w_key,
    w_value,
    w_out,
    pool_gain,
    w_in,
    block_order,
    slide_gain,
    w_sq,
    w_sk,
    w_sv,
    w_so,
):
    tile_count, patch_count, model_width = tiles.shape
    row_count = tile_count * patch_count
    inner_width = w_query.shape[1]
    normed = norm_rows(tiles, tile_gain).astype(jnp.bfloat16).reshape(row_count, model_width)
    projected = add_products(
        (normed, normed, normed),
        (
            lax.all_gather(w_query, "seq", axis=0, tiled=True),
            lax.all_gather(w_key, "seq", axis=0, tiled=True),
            lax.all_gather(w_value, "seq", axis=0, tiled=True),
        ),
    )
    tile_query, tile_keys, tile_values = (
        matrix.astype(jnp.bfloat16).reshape(tile_count, patch_count, HT, HD) for matrix in projected
    )
    scores = (
        jnp.einsum("tqhd,tkhd->thqk", tile_query, tile_keys, preferred_element_type=jnp.float32)
        * scaling
    )
    row_max = jnp.max(scores, axis=-1, keepdims=True)
    weights = jnp.exp(scores - row_max)
    totals = jnp.sum(weights, axis=-1)
    attended = jnp.einsum(
        "thqk,tkhd->tqhd",
        weights.astype(jnp.bfloat16),
        tile_values,
        preferred_element_type=jnp.float32,
    )
    attended = (attended / jnp.transpose(totals, (0, 2, 1))[..., None]).astype(jnp.bfloat16)
    attended_mean = jnp.mean(
        attended.reshape(tile_count, patch_count, inner_width), axis=1, dtype=jnp.float32
    )
    token_mean = jnp.mean(tiles, axis=1, dtype=jnp.float32)
    out_term = jnp.dot(
        attended_mean,
        lax.all_gather(w_out, "seq", axis=0, tiled=True).astype(jnp.float32),
        precision=lax.Precision.HIGHEST,
    )
    pooled = token_mean + out_term
    pooled_norm = norm_rows(pooled, pool_gain).astype(jnp.bfloat16)
    embedding = add_products((pooled_norm,), (lax.all_gather(w_in, "seq", axis=0, tiled=True),))[0]
    embedding = embedding.astype(jnp.bfloat16)
    position = lax.axis_index("seq")
    seq_size = lax.axis_size("seq")
    gathered = lax.all_gather(embedding, "seq", axis=0, tiled=True)
    slide_width = gathered.shape[1]
    block_count = block_order.shape[0]
    block_len = gathered.shape[0] // block_count
    blocks = gathered.reshape(block_count, block_len, slide_width)
    per_device = tile_count // block_len
    wanted = lax.dynamic_slice_in_dim(block_order, position * per_device, per_device)
    own_rows = jnp.take(blocks, wanted, axis=0).reshape(per_device * block_len, slide_width)
    own_norm = norm_rows(own_rows, slide_gain).astype(jnp.bfloat16)
    total_rows = seq_size * tile_count
    source_rows = own_norm.shape[0]
    slide_proj = add_products(
        (own_norm, own_norm, own_norm),
        (
            lax.all_gather(w_sq, "seq", axis=0, tiled=True),
            lax.all_gather(w_sk, "seq", axis=0, tiled=True),
            lax.all_gather(w_sv, "seq", axis=0, tiled=True),
        ),
    )
    slide_query = slide_proj[0].astype(jnp.bfloat16).reshape(tile_count, HS, HD)
    slide_keys = slide_proj[1].astype(jnp.bfloat16).reshape(source_rows, HS, HD)
    slide_values = slide_proj[2].astype(jnp.bfloat16).reshape(source_rows, HS, HD)
    head_ids = jnp.arange(HS)
    local_ids = jnp.arange(tile_count)
    level_outs = []
    level_lses = []
    level_masks = []
    for seg_len, dilation in ((total_rows // 4, 1), (total_rows // 2, 2), (total_rows, 4)):
        chosen = jnp.arange(dilation)[:, None] == head_ids[None, :] % dilation
        seg_keys = select_rows(slide_keys, chosen, dilation)
        seg_values = select_rows(slide_values, chosen, dilation)
        for bit_number in range((seg_len // tile_count).bit_length() - 1):
            other_keys, other_values = partner((seg_keys, seg_values), "seq", bit_number)
            low_half = position >> bit_number & 1 == 0
            seg_keys = jnp.where(
                low_half,
                jnp.concatenate([seg_keys, other_keys], 0),
                jnp.concatenate([other_keys, seg_keys], 0),
            )
            seg_values = jnp.where(
                low_half,
                jnp.concatenate([seg_values, other_values], 0),
                jnp.concatenate([other_values, seg_values], 0),
            )
        scores = (
            jnp.einsum("qhd,khd->hqk", slide_query, seg_keys, preferred_element_type=jnp.float32)
            * scaling
        )
        row_max = jnp.max(scores, axis=-1, keepdims=True)
        weights = jnp.exp(scores - row_max)
        totals = jnp.sum(weights, axis=-1)
        level_out = jnp.einsum(
            "hqk,khd->qhd",
            weights.astype(jnp.bfloat16),
            seg_values,
            preferred_element_type=jnp.float32,
        )
        level_outs.append(level_out / jnp.transpose(totals)[..., None])
        level_lses.append(jnp.transpose(row_max[..., 0] + jnp.log(totals)))
        level_masks.append(local_ids[:, None] % dilation == head_ids[None, :] % dilation)
    stacked_lse = jnp.stack(level_lses)
    stacked_masks = jnp.stack(level_masks)
    stacked_outs = jnp.stack(level_outs)
    best_lse = jnp.max(jnp.where(stacked_masks, stacked_lse, -jnp.inf), axis=0)
    factors = jnp.where(stacked_masks, jnp.exp(stacked_lse - best_lse[None]), 0.0)
    mixed_heads = (
        jnp.sum(factors[..., None] * stacked_outs, axis=0) / jnp.sum(factors, axis=0)[..., None]
    )
    mixed_heads = mixed_heads.astype(jnp.bfloat16).reshape(tile_count, slide_width)
    out_proj = add_products((mixed_heads,), (lax.all_gather(w_so, "seq", axis=0, tiled=True),))[0]
    return (own_rows.astype(jnp.float32) + out_proj).astype(jnp.bfloat16)


MESH = pl.DeviceIdType.MESH
f32, bf16 = jnp.float32, jnp.bfloat16


def iota(shape, dim):
    return lax.broadcasted_iota(jnp.int32, shape, dim)


def dot(a, b):
    return jnp.dot(a, b, preferred_element_type=f32)


def dot_t(a, b):
    return lax.dot_general(a, b, (((1,), (1,)), ((), ())), preferred_element_type=f32)


def attend(query, keys, values, mask=None):
    scores = dot_t(query, keys) * scaling
    if mask is not None:
        scores = jnp.where(mask, scores, -1e30)
    row_max = jnp.max(scores, axis=-1, keepdims=True)
    weights = jnp.exp(scores - row_max)
    if mask is not None:
        weights = jnp.where(mask, weights, 0.0)
    totals = jnp.sum(weights, axis=-1, keepdims=True)
    return dot(weights.astype(bf16), values) / totals, row_max + jnp.log(totals)


CHUNKS = (
    (0, 0, 384), (1, 0, 384), (2, 0, 384), (0, 384, 384), (1, 384, 384), (2, 384, 384),
    (3, 0, 768), (3, 768, 768), (4, 0, 384), (4, 384, 384), (5, 0, 768),
)
NCH = len(CHUNKS)
LINE = 4
SEQ = 16
LEAD = 2


def slab_kernel(
    tiles, tile_gain, w_query, w_key, w_value, w_out, pool_gain, w_in, block_order, slide_gain,
    w_sq, w_sk, w_sv, w_so, out,
    *scratch,
):
    bufs = scratch[:NCH]
    (normed, tq, tk, tv, att, emb, stage, wslide, perm, sq, sk, sv, souts, slses,
     msend, mrecv, mcat, own_rows,
     zs, zr, ys, yr, xs, xr, cs, cr, es, er, ws, wr, ms, mr) = scratch[NCH:]
    sources = (w_query, w_key, w_value, w_out, w_in, w_so)
    x = lax.axis_index("groups")
    me = lax.axis_index("seq")
    z = me // 4
    y = (me // 2) % 2
    c = me % 2
    at_y = {"seq": z * 4 + (1 - y) * 2 + c}
    at_c = {"seq": z * 4 + y * 2 + (1 - c)}
    at_x = {"groups": 1 - x}

    barrier = pltpu.get_barrier_semaphore()
    for o in range(1, SEQ):
        pl.semaphore_signal(barrier, inc=1, device_id={"seq": lax.rem(me + o, SEQ)}, device_id_type=MESH)
    pl.semaphore_signal(barrier, inc=1, device_id=at_x, device_id_type=MESH)

    for k, (w, first, cols) in enumerate(CHUNKS):
        bufs[k][z, y, c] = sources[w][:, first:first + cols]
    pl.semaphore_wait(barrier, SEQ)

    def copy(source, target, send, recv, device):
        return pltpu.make_async_remote_copy(
            src_ref=source, dst_ref=target, send_sem=send, recv_sem=recv,
            device_id=device, device_id_type=MESH,
        )

    def line_copy(k, way, s):
        block = z - (s - 1) if way == 0 else z + (s - 1)
        device = {"seq": me + 4} if way == 0 else {"seq": me - 4}
        valid = jnp.logical_and(z >= s - 1, z < LINE - 1) if way == 0 else jnp.logical_and(z <= LINE - s, z > 0)
        ref = bufs[k].at[block, y, c]
        n = way * 3 + s - 1
        return valid, copy(ref, ref, zs.at[k, n], zr.at[k, n], device)

    def line_send(k, s):
        for way in (0, 1):
            valid, remote = line_copy(k, way, s)
            pl.when(valid)(remote.start)

    def line_wait_send(k, s):
        for way in (0, 1):
            valid, remote = line_copy(k, way, s)
            pl.when(valid)(remote.wait_send)

    def line_wait(k, s):
        for way in (0, 1):
            valid = z >= s if way == 0 else z <= LINE - 1 - s
            block = z - s if way == 0 else z + s
            n = way * 3 + s - 1
            ref = bufs[k].at[block, y, c]
            pl.when(valid)(copy(ref, ref, zs.at[k, n], zr.at[k, n], {"seq": me}).wait_recv)

    def half(k, which_y, core, g):
        rows, cols = bufs[k].shape[3:]
        if rows % 32 == 0:
            return bufs[k].at[:, which_y, core, pl.ds(pl.multiple_of(g * (rows // 2), 16), rows // 2), :]
        return bufs[k].at[:, which_y, core, :, pl.ds(pl.multiple_of(g * (cols // 2), 128), cols // 2)]

    def y_copy(k):
        ref = half(k, y, c, x)
        return copy(ref, ref, ys.at[k], yr.at[k], at_y)

    def x_copy(k):
        ref = half(k, 1 - y, c, x)
        return copy(ref, ref, xs.at[k], xr.at[k], at_x)

    def c_copy(k, n):
        ref = bufs[k].at[:, y if n == 0 else 1 - y, c]
        return copy(ref, ref, cs.at[k, n], cr.at[k, n], at_c)

    def step(k, st):
        if st == 0:
            line_send(k, 1)
        elif st == 1:
            line_wait(k, 1)
            line_send(k, 2)
        elif st == 2:
            line_wait(k, 2)
            line_send(k, 3)
        elif st == 3:
            line_wait(k, 3)
            y_copy(k).start()
            c_copy(k, 0).start()
        elif st == 4:
            y_copy(k).wait_recv()
            x_copy(k).start()
        elif st == 5:
            x_copy(k).wait_recv()
            c_copy(k, 1).start()
        else:
            c_copy(k, 0).wait_recv()
            c_copy(k, 1).wait_recv()

    def tick(t):
        if t + LEAD < NCH:
            step(t + LEAD, 0)
        for st in range(1, 7):
            if 0 <= t - st < NCH:
                step(t - st, st)

    def weight(k):
        rows, cols = bufs[k].shape[3:]
        return bufs[k][...].reshape(SEQ * rows, cols)

    def norm_piece(first, rows):
        @pl.loop(first, first + rows, step=64)
        def _(r):
            at = pl.ds(pl.multiple_of(r, 64), 64)
            normed[at, :] = norm_rows(tiles[at, :], tile_gain[...]).astype(bf16)

    def project(k, ref):
        @pl.loop(0, 512, step=128)
        def _(r):
            at = pl.ds(pl.multiple_of(r, 128), 128)
            ref[at, :] = dot(normed[at, :], weight(k)).astype(bf16)

    def tile_attention(part, r):
        mask = iota((128, 128), 0) // 16 == iota((128, 128), 1) // 16
        at = slice(r * 128, r * 128 + 128)
        for pair in range(3):
            outs = []
            for h in (2 * pair, 2 * pair + 1):
                cols = slice(h * 64, h * 64 + 64)
                outs.append(attend(tq[part, at, cols], tk[part, at, cols], tv[part, at, cols], mask)[0])
            first = part * 384 + pair * 128
            att[at, first:first + 128] = jnp.concatenate(outs, axis=1).astype(bf16)

    def stage_slide():
        for h in range(HS):
            stage[h] = jnp.concatenate([w[:, h * 64:h * 64 + 64] for w in (w_sq, w_sk, w_sv)], axis=1)

        @pl.when(me < HS)
        def _():
            wslide[me] = stage[me]

    def w_copy(o, device, block):
        return copy(stage.at[block], wslide.at[me], ws.at[o], wr.at[o], {"seq": device})

    def slide_send(wait):
        for o in range(1, SEQ):
            d = lax.rem(me + o, SEQ)
            @pl.when(d < HS)
            def _():
                remote = w_copy(o, d, d)
                remote.wait_send() if wait else remote.start()

    def slide_wait():
        @pl.when(me < HS)
        def _():
            for o in range(1, SEQ):
                source = lax.rem(me + SEQ - o, SEQ)
                copy(stage.at[0], wslide.at[source], ws.at[o], wr.at[o], {"seq": me}).wait_recv()

    def source_rows(position):
        rows = position.shape[0]
        table = block_order[...].astype(f32)
        hot = iota((rows, 128), 1) == position[:, :1] // 4
        block = jnp.sum(jnp.where(hot, table, 0.0), axis=1, keepdims=True)
        source = block.astype(jnp.int32) * 4 + position[:, :1] % 4
        return (iota((rows, 512), 1) == source).astype(f32).astype(bf16)

    def build_perm():
        for j in range(4):
            perm[j * 128:j * 128 + 128, :] = source_rows(iota((128, 128), 0) * 4 + j)

    def e_copy(n, part, device, ref):
        ref = ref.at[..., pl.ds(384 * part, 384)]
        return copy(ref, ref, es.at[part, n], er.at[part, n], device)

    sends = []

    def emb_part(part):
        emb[z, y, c, :, 384 * part:384 * part + 384] = dot(pooled_norm, weight(8 + part)).astype(bf16)
        for o in range(1, LINE):
            sends.append(e_copy(o, part, {"seq": lax.rem(me + 4 * o, SEQ)}, emb.at[z, y, c]))
            sends[-1].start()

    def emb_line_wait(part):
        for o in range(1, LINE):
            e_copy(o, part, {"seq": me}, emb.at[lax.rem(z + LINE - o, LINE), y, c]).wait_recv()
        sends.append(e_copy(0, part, at_y, emb.at[:, y, c]))
        sends[-1].start()
        sends.append(e_copy(4, part, at_c, emb.at[:, y, c]))
        sends[-1].start()

    def emb_y_wait(part):
        e_copy(0, part, at_y, emb.at[:, 1 - y, c]).wait_recv()
        sends.append(e_copy(5, part, at_c, emb.at[:, 1 - y, c]))
        sends[-1].start()

    def emb_wait(part):
        e_copy(4, part, at_c, emb.at[:, y, 1 - c]).wait_recv()
        e_copy(5, part, at_c, emb.at[:, 1 - y, 1 - c]).wait_recv()

    for k in range(LEAD):
        step(k, 0)
    pieces = {
        8: [(0, 0)], 9: [(0, 1)], 10: [(0, 2), (0, 3)], 11: [(1, 0)], 12: [(1, 1), (1, 2)], 13: [(1, 3)],
    }
    for t in range(NCH + 5):
        tick(t)
        if t < 4:
            norm_piece(t * 128, 128)
        if t == 4:
            stage_slide()
        if t == 5:
            build_perm()
        if t == NCH - LEAD:
            slide_send(False)
        if t in (6, 9):
            project(t - 6, tq.at[(t - 6) // 3])
        if t in (7, 10):
            project(t - 6, tk.at[(t - 6) // 3])
        if t in (8, 11):
            project(t - 6, tv.at[(t - 6) // 3])
        for part, r in pieces.get(t, ()):
            tile_attention(part, r)
        if t == 12:
            gather16 = (iota((32, 512), 1) // 16 == iota((32, 512), 0)).astype(f32).astype(bf16)
            token_mean = dot(gather16, tiles[...]) * (1.0 / 16.0)
        if t == 13:
            mean = dot(gather16, att[...]) * (1.0 / 16.0)
            high = mean.astype(bf16)
            low = (mean - high.astype(f32)).astype(bf16)
            both = jnp.concatenate([high, low], axis=0)
            product = jnp.concatenate([dot(both, weight(6)), dot(both, weight(7))], axis=1)
            pooled = token_mean + product[:32] + product[32:]
            pooled_norm = norm_rows(pooled, pool_gain[...]).astype(bf16)
        if t == 14:
            emb_part(0)
        if t == 15:
            emb_part(1)
            emb_line_wait(0)
    emb_line_wait(1)
    emb_y_wait(0)
    emb_y_wait(1)
    slide_wait()
    emb_wait(0)
    emb_wait(1)

    every = emb[...].reshape(512, 768)
    own_rows[...] = dot(source_rows(iota((32, 128), 0) + me * 32), every)

    @pl.when(me < HS)
    def _():
        @pl.loop(0, 512, step=128)
        def _(r):
            at = pl.ds(pl.multiple_of(r, 128), 128)
            ordered = dot(perm[at, :], every)
            rows = norm_rows(ordered, slide_gain[...]).astype(bf16)
            projected = dot(rows, wslide[...].reshape(768, 192)).astype(bf16)
            sq[at, :] = projected[:, :64]
            sk[at, :] = projected[:, 64:128]
            sv[at, :] = projected[:, 128:]

        for level in (1, 2):
            slses[level] = jnp.full((512, 64), -1e30, f32)
            souts[level] = jnp.zeros((512, 64), f32)

        def level_attention(level, pieces):
            def rows(ref):
                return jnp.concatenate([ref[at, :] for at in pieces], axis=0)
            result, lse = attend(rows(sq), rows(sk), rows(sv))
            lse = jnp.broadcast_to(lse, result.shape)
            size = 128 // len(pieces)
            for n, at in enumerate(pieces):
                souts[level, at, :] = result[n * size:n * size + size]
                slses[level, at, :] = lse[n * size:n * size + size]

        for s in range(4):
            level_attention(0, [pl.ds(j * 128 + 32 * s, 32) for j in range(4)])
        even = (me % 2) * 128
        for s in range(2):
            level_attention(1, [pl.ds(pl.multiple_of(even + j * 256 + 64 * s, 64), 64) for j in range(2)])
        level_attention(2, [pl.ds(pl.multiple_of((me % 4) * 128, 128), 128)])
        best = jnp.maximum(jnp.maximum(slses[0], slses[1]), slses[2])
        total = jnp.zeros((512, 64), f32)
        mixed = jnp.zeros((512, 64), f32)
        for level in range(3):
            factor = jnp.exp(slses[level] - best)
            total = total + factor
            mixed = mixed + factor * souts[level]
        mixed = (mixed / total).astype(bf16)
        rows, cols = iota((512, 512), 0), iota((512, 512), 1)
        back = (cols == (rows % 4) * 128 + rows // 4).astype(f32).astype(bf16)
        msend[...] = dot(back, mixed).astype(bf16).reshape(SEQ, 32, 64)
        mrecv[me] = msend[me]
        for o in range(1, SEQ):
            d = lax.rem(me + o, SEQ)
            copy(msend.at[d], mrecv.at[me], ms.at[o], mr.at[o], {"seq": d}).start()

    for o in range(1, SEQ):
        source = lax.rem(me + SEQ - o, SEQ)
        pl.when(source < HS)(copy(msend.at[0], mrecv.at[jnp.minimum(source, HS - 1)], ms.at[o], mr.at[o], {"seq": me}).wait_recv)
    for h in range(HS):
        mcat[:, h * 64:h * 64 + 64] = mrecv[h]
    step(NCH - 1, 6)
    out[...] = (own_rows[...] + dot(mcat[...], weight(10))).astype(bf16)

    @pl.when(me < HS)
    def _():
        for o in range(1, SEQ):
            d = lax.rem(me + o, SEQ)
            copy(msend.at[d], mrecv.at[me], ms.at[o], mr.at[o], {"seq": d}).wait_send()
    slide_send(True)
    for remote in sends:
        remote.wait_send()
    for k in range(NCH):
        for s in range(1, LINE):
            line_wait_send(k, s)
        y_copy(k).wait_send()
        x_copy(k).wait_send()
        c_copy(k, 0).wait_send()
        c_copy(k, 1).wait_send()


def shards_in_kernel(tiles, tile_gain, w_query, w_key, w_value, w_out, pool_gain, w_in, block_order,
                     slide_gain, w_sq, w_sk, w_sv, w_so):
    weights = (w_query, w_key, w_value, w_out, w_in, w_so)
    vmem, dma = pltpu.VMEM, pltpu.SemaphoreType.DMA
    scratch = [vmem((LINE, 2, 2, weights[w].shape[0], cols), bf16) for w, _, cols in CHUNKS]
    scratch += [
        vmem((512, 1536), bf16),
        vmem((2, 512, 384), bf16), vmem((2, 512, 384), bf16), vmem((2, 512, 384), bf16),
        vmem((512, 768), bf16),
        vmem((LINE, 2, 2, 32, 768), bf16),
        vmem((HS, 48, 192), bf16), vmem((SEQ, 48, 192), bf16),
        vmem((512, 512), bf16),
        vmem((512, 64), bf16), vmem((512, 64), bf16), vmem((512, 64), bf16),
        vmem((3, 512, 64), f32), vmem((3, 512, 64), f32),
        vmem((SEQ, 32, 64), bf16), vmem((HS, 32, 64), bf16), vmem((32, 768), bf16),
        vmem((32, 768), f32),
        dma((NCH, 6)), dma((NCH, 6)), dma((NCH,)), dma((NCH,)), dma((NCH,)), dma((NCH,)),
        dma((NCH, 2)), dma((NCH, 2)), dma((2, 6)), dma((2, 6)),
        dma((SEQ,)), dma((SEQ,)), dma((SEQ,)), dma((SEQ,)),
    ]
    return pl.pallas_call(
        slab_kernel,
        out_shape=jax.ShapeDtypeStruct((32, 768), bf16),
        in_specs=[pl.BlockSpec(memory_space=pltpu.VMEM)] * 14,
        out_specs=pl.BlockSpec(memory_space=pltpu.VMEM),
        scratch_shapes=scratch,
        compiler_params=pltpu.CompilerParams(
            collective_id=0, has_side_effects=True, vmem_limit_bytes=56 * 1024 * 1024
        ),
        cost_estimate=pl.CostEstimate(flops=6 * 10**9, bytes_accessed=4 * 10**6, transcendentals=10**6),
        name="slab",
    )(
        tiles.reshape(512, 1536), tile_gain, w_query, w_key, w_value, w_out,
        pool_gain, w_in, block_order.reshape(1, -1), slide_gain,
        w_sq, w_sk, w_sv, w_so,
    )


def solution(mesh):
    shards = shards_by_gathers
    if mesh.shape['groups'] == 2 and mesh.shape['seq'] == 16:
        shards = shards_in_kernel

    placed = (
        P(("groups", "seq"), None, None),
        P(),
        P("seq", None),
        P("seq", None),
        P("seq", None),
        P("seq", None),
        P(),
        P("seq", None),
        P("groups"),
        P(),
        P("seq", None),
        P("seq", None),
        P("seq", None),
        P("seq", None),
    )
    return jax.shard_map(
        shards, mesh=mesh, in_specs=placed, out_specs=P(("groups", "seq"), None), check_vma=False
    )
```
